256 devices in a mesh: row: 16 (over z_lo, y, core), col: 16 (over x, z_hi).
Axes of the slice: x: 4, y: 4, z: 8 (z_hi: 4, z_lo: 2; z = z_hi * 2 + z_lo), core: 2. Of those that a mesh axis runs over, the one named last changes fastest.
Arguments:
- tile_values: bfloat16 [16, 16, 320, 128, 128], P('row', 'col')
- tile_rows: int32 [16, 16, 320], P('row', 'col'), may hold values from 0 to 511
- tile_cols: int32 [16, 16, 320], P('row', 'col'), may hold values from 0 to 255
- tile_counts: int32 [16, 16], P('row', 'col'), may hold values from 160 to 320, as said below
- solution: float32 [4, 524288], P(None, ('col', 'row')), may hold values from -6 to 6
- residual: float32 [4, 1048576], P(None, ('row', 'col')), may hold values from -6 to 6
- direction: float32 [4, 524288], P(None, ('col', 'row')), may hold values from -6 to 6
- grad_norm: float32 [4], replicated, may hold values from 314572.8 to 3145728
Outputs:
- new_solution: float32 [4, 524288], P(None, ('col', 'row'))
- new_residual: float32 [4, 1048576], P(None, ('row', 'col'))
- new_direction: float32 [4, 524288], P(None, ('col', 'row'))
The draws below stay inside these ranges and needn't reach their ends.
Inputs may be any that keep to these rules, and one draw needn't show every extreme that they name: Each device uses its first tile_counts slots; at least half of 320, and some device uses all 320.
All inputs are finite; a program needn't handle non-finite values.
Results may differ from the reference program's by a relative error of at most 0.0032.
Values may be sent and summed in bfloat16 or wider, within the bound.
A program may use at most 128 MiB of HBM per device.

```python
import math
import jax
import jax.numpy as jnp
from jax import lax

TB = 128
RHS = 4
BR = 512
BC = 256
K_TILES = 320
ROWS = 1048576
COLS = 524288
N_ROW = 16
N_COL = 16


def draw_tile_values(key, part):
    key = jax.random.fold_in(key, 7)
    fan_total = TB * N_COL * 0.75 * K_TILES / BR
    row_pos = jnp.arange(N_ROW, dtype=jnp.float32) / max(N_ROW - 1, 1)
    col_pos = jnp.arange(N_COL, dtype=jnp.float32) / max(N_COL - 1, 1)
    shape_all = (N_ROW, N_COL, K_TILES, TB, TB)
    base = jax.random.normal(key, shape_all, jnp.float32)
    row_scale = jnp.exp(jnp.log(3.0) * (0.5 * row_pos - 0.25))
    col_scale = jnp.exp(jnp.log(3.0) * (0.5 * col_pos - 0.25))
    factor = row_scale[:, None] * col_scale[None, :]
    values = base * factor[:, :, None, None, None] / jnp.sqrt(fan_total)
    return values.astype(jnp.bfloat16)


def draw_tile_counts(key, part):
    key = jax.random.fold_in(key, 5)
    first_key, second_key = jax.random.split(key)
    drawn = jax.random.randint(first_key, (N_ROW * N_COL,), K_TILES // 2, K_TILES + 1, dtype=jnp.int32)
    full_slot = jax.random.randint(second_key, (), 0, N_ROW * N_COL, dtype=jnp.int32)
    drawn = drawn.at[full_slot].set(K_TILES)
    return drawn.reshape(N_ROW, N_COL)


def with_ends(array, stream_key, smallest, top_value):
    shape = array.shape
    spot = [jax.random.randint(jax.random.fold_in(stream_key, axis), (), 0, shape[axis]) for axis in range(len(shape))]
    array = array.at[tuple(spot)].set(smallest)
    longest = shape.index(max(shape))
    spot[longest] = (spot[longest] + 1) % shape[longest]
    return array.at[tuple(spot)].set(top_value)


def shard_levels(own_key, extent, shards, least, high):
    gain, own = 1.0, jax.random.fold_in(own_key, 6)
    for position, parts in shards:
        draws = jnp.exp(jax.random.uniform(jax.random.fold_in(own, position), (parts,), jnp.float32, least / len(shards), high / len(shards)))
        gain = gain * jnp.repeat(draws, extent[position] // parts).reshape([-1 if axis == position else 1 for axis in range(len(extent))])
    return gain


def bell_draw(rng, extent, spread, reach, cuts=(), kind=jnp.bfloat16):
    result = jax.random.normal(rng, extent, jnp.float32) * spread
    if len(cuts) > 0:
        result = shard_levels(rng, extent, cuts, -0.22, 0.18) * result
    return jnp.clip(result, min=-reach, max=reach).astype(kind)


def setup_inputs(seed: int = 0) -> dict:
    arg_keys = jax.random.split(jax.random.key(seed), 9)
    return {
        "tile_values": draw_tile_values(jax.random.fold_in(arg_keys[8], 71), 0),
        "tile_rows": with_ends(jax.random.randint(arg_keys[1], (N_ROW, N_COL, K_TILES), 0, BR), jax.random.fold_in(arg_keys[1], 1), 0, BR - 1).astype(jnp.int32),
        "tile_cols": with_ends(jax.random.randint(arg_keys[2], (N_ROW, N_COL, K_TILES), 0, BC), jax.random.fold_in(arg_keys[2], 1), 0, BC - 1).astype(jnp.int32),
        "tile_counts": draw_tile_counts(jax.random.fold_in(arg_keys[8], 71), 0),
        "solution": bell_draw(arg_keys[4], (RHS, COLS), 1.0, 6.0, ((1, 256),), jnp.float32),
        "residual": bell_draw(arg_keys[5], (RHS, ROWS), 1.0, 6.0, ((1, 256),), jnp.float32),
        "direction": bell_draw(arg_keys[6], (RHS, COLS), 1.0, 6.0, ((1, 256),), jnp.float32),
        "grad_norm": jnp.clip(jnp.exp(jax.random.uniform(arg_keys[7], (RHS,), jnp.float32, math.log(314572.8), math.log(3145728))), 314572.8, 3145728),
    }


def apply_blocks(tile_values, tile_rows, tile_cols, tile_counts, vector, transpose_dir):
    device_total = N_ROW * N_COL
    flat_tiles = tile_values.reshape(device_total, K_TILES, TB, TB)
    flat_rows = tile_rows.reshape(device_total, K_TILES)
    flat_cols = tile_cols.reshape(device_total, K_TILES)
    flat_counts = tile_counts.reshape(device_total)
    if transpose_dir:
        blocks_in = vector.reshape(RHS, BR * N_ROW, TB)
        blocks_out = BC * N_COL
    else:
        blocks_in = vector.reshape(RHS, BC * N_COL, TB)
        blocks_out = BR * N_ROW

    def add_device(running, device_index):
        row_group = device_index // N_COL
        col_group = device_index % N_COL
        tiles_here = flat_tiles[device_index].astype(jnp.float32)
        rows_here = flat_rows[device_index] + row_group * BR
        cols_here = flat_cols[device_index] + col_group * BC
        slot_used = (jnp.arange(K_TILES, dtype=jnp.int32) < flat_counts[device_index]).astype(jnp.float32)
        if transpose_dir:
            picked = blocks_in[:, rows_here, :].astype(jnp.float32)
            contrib = jnp.einsum('kab,rka->krb', tiles_here, picked, precision=lax.Precision.HIGHEST)
            target = cols_here
        else:
            picked = blocks_in[:, cols_here, :].astype(jnp.float32)
            contrib = jnp.einsum('kab,rkb->kra', tiles_here, picked, precision=lax.Precision.HIGHEST)
            target = rows_here
        contrib = contrib * slot_used[:, None, None]
        return running + jax.ops.segment_sum(contrib, target, num_segments=blocks_out), None

    start_blocks = jnp.zeros((blocks_out, RHS, TB), jnp.float32)
    running, _ = lax.scan(add_device, start_blocks, jnp.arange(device_total, dtype=jnp.int32))
    return jnp.moveaxis(running, 0, 1).reshape(RHS, blocks_out * TB)


def reference(tile_values, tile_rows, tile_cols, tile_counts, solution, residual, direction, grad_norm):
    direction_low = direction.astype(jnp.bfloat16)
    image = apply_blocks(tile_values, tile_rows, tile_cols, tile_counts, direction_low, False)
    curvature = jnp.sum(image * image, axis=1)
    step_len = grad_norm / curvature
    new_solution = solution + step_len[:, None] * direction
    new_residual = residual - step_len[:, None] * image
    residual_low = new_residual.astype(jnp.bfloat16)
    gradient = apply_blocks(tile_values, tile_rows, tile_cols, tile_counts, residual_low, True)
    norm_next = jnp.sum(gradient * gradient, axis=1)
    beta_ratio = norm_next / grad_norm
    new_direction = gradient + beta_ratio[:, None] * direction
    return (new_solution, new_residual, new_direction)
```

```python
import jax
import jax.numpy as jnp
from jax import lax
from jax.experimental import pallas as pl
from jax.experimental.pallas import tpu as pltpu
from jax.sharding import PartitionSpec as P

TB = 128
RHS = 4
BR = 512
BC = 256
K = 320
HALF = K // 2
KPAD = 384
NG = 16
NX = 4
NZ = 4
PR = BR // NG
PC = BC // NG
F32 = jnp.float32
BF16 = jnp.bfloat16
MESH = pl.DeviceIdType.MESH


def remote(src, dst, send_sem, recv_sem, device):
    return pltpu.make_async_remote_copy(
        src_ref=src,
        dst_ref=dst,
        send_sem=send_sem,
        recv_sem=recv_sem,
        device_id=device,
        device_id_type=MESH,
    )


def turn(base, step, size):
    return lax.rem(base + step + size, size)


def repeat(count, body, unroll=1):
    def step(index, carry):
        body(index)
        return carry

    lax.fori_loop(0, count, step, 0, unroll=unroll)


def kernel(
    count_s, rows_s, cols_s, gamma_s, rows_v, cols_v, tiles, sol, res, dirn,
    out_sol, out_res, out_dir,
    t, xg, ag, rg, sb, r1, r2, gs, gr, dpiece, rpiece, image, xf, rf, ys, hilo, hit_r, hit_c,
    grad_r, idx, ca, cb, na, nb,
    t_sem, x_ss, x_rs, rz_ss, rz_rs, rx_ss, rx_rs, s1_ss, s1_rs, s2_ss, s2_rs,
    az_ss, az_rs, ax_ss, ax_rs, g_ss, g_rs, ca_ss, ca_rs, cb_ss, cb_rs, na_ss, na_rs, nb_ss, nb_rs,
):
    i = lax.axis_index("row")
    j = lax.axis_index("col")
    x = j // NZ
    z = lax.rem(j, NZ)

    def row_peer(d):
        return (turn(i, d, NG), j)

    def col_peer(d):
        return (i, turn(j, d, NG))

    def x_peer(d):
        return (i, turn(x, d, NX) * NZ + z)

    def z_peer(d):
        return (i, x * NZ + turn(z, d, NZ))

    def tile_copy(c):
        part = pl.ds(c * (K // 4), K // 4)
        return pltpu.make_async_copy(tiles.at[0, 0, part], t.at[part], t_sem.at[c])

    for c in range(4):
        tile_copy(c).start()

    for buf in (ca, cb, na, nb):
        buf[...] = jnp.zeros_like(buf)

    barrier = pltpu.get_barrier_semaphore()

    def greet(d):
        pl.semaphore_signal(barrier, inc=1, device_id=row_peer(d + 1), device_id_type=MESH)
        pl.semaphore_signal(barrier, inc=1, device_id=col_peer(d + 1), device_id_type=MESH)

    repeat(NG - 1, greet)

    def cut_dir(b):
        for r in range(RHS):
            dpiece[r, pl.ds(b, 1), :] = dirn[pl.ds(r, 1), pl.ds(pl.multiple_of(b * TB, TB), TB)]

    def cut_res(b):
        for r in range(RHS):
            rpiece[r, pl.ds(b, 1), :] = res[pl.ds(r, 1), pl.ds(pl.multiple_of(b * TB, TB), TB)]

    repeat(PC, cut_dir, unroll=4)
    xg[i] = dpiece[...].astype(BF16)
    repeat(PR, cut_res, unroll=4)
    rg[j] = rpiece[...].astype(BF16)

    pl.semaphore_wait(barrier, 2 * (NG - 1))

    def send_x(d):
        return remote(xg.at[i], xg.at[i], x_ss.at[d], x_rs.at[d], row_peer(d + 1))

    def take_x(d):
        s = turn(i, -d - 1, NG)
        return remote(xg.at[s], xg.at[s], x_ss.at[d], x_rs.at[d], row_peer(d + 1))

    def z_send(buf, ss, rs, d):
        return remote(buf.at[j], buf.at[j], ss.at[d], rs.at[d], z_peer(d + 1))

    def z_take(buf, ss, rs, d):
        s = x * NZ + turn(z, -d - 1, NZ)
        return remote(buf.at[s], buf.at[s], ss.at[d], rs.at[d], z_peer(d + 1))

    def x_send(buf, ss, rs, e, d):
        s = x * NZ + turn(z, -e, NZ)
        return remote(buf.at[s], buf.at[s], ss.at[e, d], rs.at[e, d], x_peer(d + 1))

    def x_take(buf, ss, rs, e, d):
        s = turn(x, -d - 1, NX) * NZ + turn(z, -e, NZ)
        return remote(buf.at[s], buf.at[s], ss.at[e, d], rs.at[e, d], x_peer(d + 1))

    def gather_first(buf, zs, zr, xs, xr):
        repeat(NZ - 1, lambda d: z_send(buf, zs, zr, d).start())
        repeat(NX - 1, lambda d: x_send(buf, xs, xr, 0, d).start())

    def gather_forward(buf, zs, zr, xs, xr):
        def forward(d):
            z_take(buf, zs, zr, d).wait_recv()
            repeat(NX - 1, lambda f: x_send(buf, xs, xr, d + 1, f).start())

        repeat(NZ - 1, forward)

    def gather_last(buf, zs, zr, xs, xr):
        repeat(NZ, lambda e: repeat(NX - 1, lambda d: x_take(buf, xs, xr, e, d).wait_recv()))

    def gather_sent(buf, zs, zr, xs, xr):
        repeat(NZ - 1, lambda d: z_send(buf, zs, zr, d).wait_send())
        repeat(NZ, lambda e: repeat(NX - 1, lambda d: x_send(buf, xs, xr, e, d).wait_send()))

    repeat(NG - 1, lambda d: send_x(d).start())
    old = (rg, rz_ss, rz_rs, rx_ss, rx_rs)
    new = (ag, az_ss, az_rs, ax_ss, ax_rs)
    gather_first(*old)

    idx[...] = jnp.zeros_like(idx)
    idx[0:1, 0:K] = rows_v[0]
    idx[1:2, 0:K] = cols_v[0]
    count = count_s[0, 0]
    used = lax.broadcasted_iota(jnp.int32, (TB, KPAD), 1) < count
    down = lax.broadcasted_iota(jnp.int32, (TB, KPAD), 0)
    for c in range(BR // TB):
        hit = jnp.where((down + c * TB == idx[0:1, :]) & used, 1.0, 0.0).astype(BF16)
        hit_r[c * TB : (c + 1) * TB, 0:KPAD] = hit
        hit_r[c * TB : (c + 1) * TB, KPAD : 2 * KPAD] = hit
    for c in range(BC // TB):
        hit = jnp.where((down + c * TB == idx[1:2, :]) & used, 1.0, 0.0).astype(BF16)
        hit_c[c * TB : (c + 1) * TB, 0:KPAD] = hit
        hit_c[c * TB : (c + 1) * TB, KPAD : 2 * KPAD] = hit
    hilo[K:KPAD, :] = jnp.zeros((KPAD - K, RHS * TB), BF16)
    hilo[KPAD + K :, :] = jnp.zeros((KPAD - K, RHS * TB), BF16)

    top = lax.broadcasted_iota(jnp.int32, (8, TB), 0) < RHS
    slot = lax.broadcasted_iota(jnp.int32, (HALF, TB), 0)

    def spread(src, dst, p, blocks):
        at = pl.ds(pl.multiple_of(p * blocks, blocks), blocks)
        for r in range(RHS):
            v = src[p, r].astype(F32)
            dst[at, r, :] = v
            dst[at, RHS + r, :] = v

    def products(vec, index_s, transpose):
        axis = 0 if transpose else 1

        def pair(k):
            a = vec[index_s[0, 0, k]]
            b = vec[index_s[0, 0, k + HALF]]
            lhs = jnp.concatenate([jnp.where(top, a, 0.0), jnp.where(top, 0.0, b)], axis=1)
            rhs = jnp.concatenate([t[k], t[k + HALF]], axis=axis)
            ys[k] = lax.dot_general(
                lhs.astype(BF16), rhs, (((1,), (axis,)), ((), ())), preferred_element_type=F32
            )

        repeat(HALF, pair, unroll=8)
        for h in range(2):
            live = slot + h * HALF < count
            at = pl.ds(h * HALF, HALF)
            low_at = pl.ds(KPAD + h * HALF, HALF)
            for r in range(RHS):
                y = jnp.where(live, ys[:, h * RHS + r, :], 0.0)
                high = y.astype(BF16)
                hilo[at, r * TB : (r + 1) * TB] = high
                hilo[low_at, r * TB : (r + 1) * TB] = (y - high.astype(F32)).astype(BF16)

    def take_dir(d):
        take_x(d).wait_recv()
        spread(xg, xf, turn(i, -d - 1, NG), PC)

    spread(xg, xf, i, PC)
    repeat(NG - 1, take_dir)
    gather_forward(*old)
    for c in range(4):
        tile_copy(c).wait()
    products(xf, cols_s, False)

    def s1_send(d, e):
        p = turn(x, d + 1, NX) * NZ + turn(z, e + 1, NZ)
        dst = r1.at[turn(z, e + 1, NZ), x]
        return remote(sb.at[p], dst, s1_ss.at[d, e], s1_rs.at[d, e], x_peer(d + 1))

    def s1_take(d, e):
        dst = r1.at[turn(z, e + 1, NZ), turn(x, -d - 1, NX)]
        return remote(dst, dst, s1_ss.at[d, e], s1_rs.at[d, e], x_peer(d + 1))

    def s2_send(e):
        return remote(
            sb.at[x * NZ + turn(z, e + 1, NZ)], r2.at[z], s2_ss.at[e], s2_rs.at[e], z_peer(e + 1)
        )

    def s2_take(e):
        dst = r2.at[turn(z, -e - 1, NZ)]
        return remote(dst, dst, s2_ss.at[e], s2_rs.at[e], z_peer(e + 1))

    def image_chunk(d):
        xd = turn(x, d + 1, NX)
        hit = hit_r[pl.ds(pl.multiple_of(xd * TB, TB), TB), :]
        part = lax.dot_general(hit, hilo[...], (((1,), (0,)), ((), ())), preferred_element_type=F32)
        for q in range(NZ):
            for r in range(RHS):
                sb[xd * NZ + q, r] = part[q * PR : (q + 1) * PR, r * TB : (r + 1) * TB].astype(BF16)

    def image_out(d):
        image_chunk(d)
        repeat(NZ, lambda e: s1_send(d, e).start())

    repeat(NX - 1, image_out)
    image_chunk(NX - 1)

    spread(rg, rf, j, PR)

    def take_res(e):
        def one(d):
            x_take(*((rg,) + old[3:]), e, d).wait_recv()
            spread(rg, rf, turn(x, -d - 1, NX) * NZ + turn(z, -e, NZ), PR)

        repeat(NX - 1, one)

    repeat(NZ, take_res)
    repeat(NZ - 1, lambda d: spread(rg, rf, x * NZ + turn(z, -d - 1, NZ), PR))
    products(rf, rows_s, True)
    for c in range(BC // TB):
        grad_r[c * TB : (c + 1) * TB, :] = lax.dot_general(
            hit_c[c * TB : (c + 1) * TB, :], hilo[...], (((1,), (0,)), ((), ())),
            preferred_element_type=F32,
        )

    def over_x(e):
        zt = turn(z, e + 1, NZ)
        repeat(NX - 1, lambda d: s1_take(d, e).wait_recv())
        total = sb[x * NZ + zt].astype(F32)
        for d in range(NX - 1):
            total += r1[zt, turn(x, -d - 1, NX)].astype(F32)
        return total

    def through(e):
        sb[x * NZ + turn(z, e + 1, NZ)] = over_x(e).astype(BF16)
        s2_send(e).start()

    repeat(NZ - 1, through)
    image[...] = over_x(NZ - 1)

    def add_image(e):
        s2_take(e).wait_recv()
        image[...] += r2[turn(z, -e - 1, NZ)].astype(F32)

    repeat(NZ - 1, add_image)

    ag[j] = image[...].astype(BF16)
    gather_first(*new)

    def share(buf, me, peer, ss, rs):
        return lambda d: remote(buf.at[me], buf.at[me], ss.at[d], rs.at[d], peer(d + 1))

    def shared(buf, me, peer, ss, rs):
        def take(d):
            s = turn(me, -d - 1, NG)
            remote(buf.at[s], buf.at[s], ss.at[d], rs.at[d], peer(d + 1)).wait_recv()

        repeat(NG - 1, take)
        return jnp.sum(buf[...], axis=0)

    for r in range(RHS):
        v = image[r]
        ca[j, r : r + 1, :] = jnp.sum(v * v, axis=0, keepdims=True)
    c_col = (ca, j, col_peer, ca_ss, ca_rs)
    c_row = (cb, i, row_peer, cb_ss, cb_rs)
    repeat(NG - 1, lambda d: share(*c_col)(d).start())
    gather_forward(*new)
    cb[i] = shared(*c_col)
    repeat(NG - 1, lambda d: share(*c_row)(d).start())

    line = lax.broadcasted_iota(jnp.int32, (RHS, 1), 0)
    gamma = jnp.full((RHS, 1), gamma_s[0], F32)
    for r in range(1, RHS):
        gamma = jnp.where(line == r, gamma_s[r], gamma)

    curvature = jnp.sum(shared(*c_row)[0:RHS, :], axis=1, keepdims=True)
    step = gamma / curvature
    out_sol[...] = sol[...] + step * dirn[...]

    def write_res(b):
        for r in range(RHS):
            at = pl.ds(pl.multiple_of(b * TB, TB), TB)
            out_res[pl.ds(r, 1), at] = (
                res[pl.ds(r, 1), at] - step[r : r + 1, :] * image[r, pl.ds(b, 1), :]
            )

    repeat(PR, write_res, unroll=4)

    spread(ag, rf, j, PR)
    repeat(NZ - 1, lambda d: spread(ag, rf, x * NZ + turn(z, -d - 1, NZ), PR))

    def take_image(e):
        def one(d):
            x_take(*((ag,) + new[3:]), e, d).wait_recv()
            spread(ag, rf, turn(x, -d - 1, NX) * NZ + turn(z, -e, NZ), PR)

        repeat(NX - 1, one)

    repeat(NZ, take_image)
    products(rf, rows_s, True)

    def g_send(d):
        return remote(gs.at[turn(i, d + 1, NG)], gr.at[i], g_ss.at[d], g_rs.at[d], row_peer(d + 1))

    def g_take(d):
        dst = gr.at[turn(i, -d - 1, NG)]
        return remote(dst, dst, g_ss.at[d], g_rs.at[d], row_peer(d + 1))

    step_wide = jnp.concatenate(
        [jnp.broadcast_to(step[r : r + 1, :], (1, TB)) for r in range(RHS)], axis=1
    )
    for c in range(BC // TB):
        part = lax.dot_general(
            hit_c[c * TB : (c + 1) * TB, :], hilo[...], (((1,), (0,)), ((), ())),
            preferred_element_type=F32,
        )
        part = grad_r[c * TB : (c + 1) * TB, :] - step_wide * part
        for q in range(TB // PC):
            for r in range(RHS):
                gs[c * (TB // PC) + q, r] = part[
                    q * PC : (q + 1) * PC, r * TB : (r + 1) * TB
                ].astype(BF16)
    repeat(NG - 1, lambda d: g_send(d).start())

    repeat(NG - 1, lambda d: send_x(d).wait_send())
    gather_sent(*old)
    gather_sent(*new)
    repeat(NX - 1, lambda d: repeat(NZ, lambda e: s1_send(d, e).wait_send()))
    repeat(NZ - 1, lambda e: s2_send(e).wait_send())
    repeat(NG - 1, lambda d: share(*c_col)(d).wait_send())
    repeat(NG - 1, lambda d: share(*c_row)(d).wait_send())

    repeat(NG - 1, lambda d: g_take(d).wait_recv())
    gr[i] = gs[i]
    grad = gr[0].astype(F32)
    for s in range(1, NG):
        grad += gr[s].astype(F32)

    for r in range(RHS):
        v = grad[r]
        na[i, r : r + 1, :] = jnp.sum(v * v, axis=0, keepdims=True)
    n_row = (na, i, row_peer, na_ss, na_rs)
    n_col = (nb, j, col_peer, nb_ss, nb_rs)
    repeat(NG - 1, lambda d: share(*n_row)(d).start())
    nb[j] = shared(*n_row)
    repeat(NG - 1, lambda d: share(*n_col)(d).start())
    norm_next = jnp.sum(shared(*n_col)[0:RHS, :], axis=1, keepdims=True)
    beta = norm_next / gamma
    for r in range(RHS):
        full = grad[r] + beta[r : r + 1, :] * dpiece[r]
        for b in range(PC):
            out_dir[r : r + 1, b * TB : (b + 1) * TB] = full[b : b + 1, :]

    repeat(NG - 1, lambda d: g_send(d).wait_send())
    repeat(NG - 1, lambda d: share(*n_row)(d).wait_send())
    repeat(NG - 1, lambda d: share(*n_col)(d).wait_send())


def on_device(
    tile_values, tile_rows, tile_cols, tile_counts, solution, residual, direction, grad_norm
):
    smem = pl.BlockSpec(memory_space=pltpu.SMEM)
    vmem = pl.BlockSpec(memory_space=pltpu.VMEM)
    piece_r = (RHS, PR, TB)
    piece_c = (RHS, PC, TB)
    dma = pltpu.SemaphoreType.DMA
    peers = [dma((NG - 1,)), dma((NG - 1,))]
    staged = [dma((NZ - 1,)), dma((NZ - 1,)), dma((NZ, NX - 1)), dma((NZ, NX - 1))]
    return pl.pallas_call(
        kernel,
        out_shape=(
            jax.ShapeDtypeStruct(solution.shape, F32),
            jax.ShapeDtypeStruct(residual.shape, F32),
            jax.ShapeDtypeStruct(direction.shape, F32),
        ),
        in_specs=[smem, smem, smem, smem, vmem, vmem, pl.BlockSpec(memory_space=pltpu.HBM)]
        + [vmem] * 3,
        out_specs=(vmem, vmem, vmem),
        scratch_shapes=[
            pltpu.VMEM((K, TB, TB), BF16),
            pltpu.VMEM((NG,) + piece_c, BF16),
            pltpu.VMEM((NG,) + piece_r, BF16),
            pltpu.VMEM((NG,) + piece_r, BF16),
            pltpu.VMEM((NG,) + piece_r, BF16),
            pltpu.VMEM((NZ, NX) + piece_r, BF16),
            pltpu.VMEM((NZ,) + piece_r, BF16),
            pltpu.VMEM((NG,) + piece_c, BF16),
            pltpu.VMEM((NG,) + piece_c, BF16),
            pltpu.VMEM(piece_c, F32),
            pltpu.VMEM(piece_r, F32),
            pltpu.VMEM(piece_r, F32),
            pltpu.VMEM((BC, 2 * RHS, TB), F32),
            pltpu.VMEM((BR, 2 * RHS, TB), F32),
            pltpu.VMEM((HALF, 2 * RHS, TB), F32),
            pltpu.VMEM((2 * KPAD, RHS * TB), BF16),
            pltpu.VMEM((BR, 2 * KPAD), BF16),
            pltpu.VMEM((BC, 2 * KPAD), BF16),
            pltpu.VMEM((BC, RHS * TB), F32),
            pltpu.VMEM((8, KPAD), jnp.int32),
            pltpu.VMEM((NG, 8, TB), F32),
            pltpu.VMEM((NG, 8, TB), F32),
            pltpu.VMEM((NG, 8, TB), F32),
            pltpu.VMEM((NG, 8, TB), F32),
            dma((4,)),
            *peers,
            *staged,
            dma((NX - 1, NZ)), dma((NX - 1, NZ)),
            dma((NZ - 1,)), dma((NZ - 1,)),
            *staged,
            *peers,
            *peers, *peers, *peers, *peers,
        ],
        compiler_params=pltpu.CompilerParams(
            collective_id=0, has_side_effects=True, vmem_limit_bytes=60 * 1024 * 1024
        ),
    )(
        tile_counts, tile_rows, tile_cols, grad_norm, tile_rows, tile_cols,
        tile_values, solution, residual, direction,
    )


def solution(mesh):
    in_specs = (
        P("row", "col", None, None, None),
        P("row", "col", None),
        P("row", "col", None),
        P("row", "col"),
        P(None, ("col", "row")),
        P(None, ("row", "col")),
        P(None, ("col", "row")),
        P(),
    )
    out_specs = (P(None, ("col", "row")), P(None, ("row", "col")), P(None, ("col", "row")))
    return jax.shard_map(
        on_device, mesh=mesh, in_specs=in_specs, out_specs=out_specs, check_vma=False
    )
```

```python
import jax
import jax.numpy as jnp
from jax import lax
from jax.experimental import pallas as pl
from jax.experimental.pallas import tpu as pltpu
from jax.sharding import PartitionSpec as P

TB = 128
RHS = 4
BR = 512
BC = 256
K = 320
HALF = K // 2
QUARTER = K // 4
KPAD = 384
NG = 16
NX = 4
NZ = 4
FAR_FIRST = (1, 0, 2)
FAR_LAST = (0, 2, 1)
NQ = NG // 2
PR = BR // NG
PC = BC // NG
F32 = jnp.float32
BF16 = jnp.bfloat16
MESH = pl.DeviceIdType.MESH


def remote(src, dst, send_sem, recv_sem, device):
    return pltpu.make_async_remote_copy(
        src_ref=src,
        dst_ref=dst,
        send_sem=send_sem,
        recv_sem=recv_sem,
        device_id=device,
        device_id_type=MESH,
    )


def turn(base, step, size):
    return lax.rem(base + step + size, size)


def repeat(count, body, unroll=1):
    def step(index, carry):
        body(index)
        return carry

    lax.fori_loop(0, count, step, 0, unroll=unroll)


def kernel(
    count_s, rows_s, cols_s, gamma_s, rows_v, cols_v, tiles, res, dirn,
    out_image, out_grad, out_scale,
    t, xg, ag, rg, sb, r1, r2, gs, gr, dpiece, rpiece, image, xf, rf, ys, hilo, hit_r, hit_c,
    grad_r, idx, ca, cb, na, nb,
    t_sem, x_ss, x_rs, t_ss, t_rs, rz_ss, rz_rs, rx_ss, rx_rs, s1_ss, s1_rs, s2_ss, s2_rs,
    az_ss, az_rs, ax_ss, ax_rs, g_ss, g_rs, ca_ss, ca_rs, cb_ss, cb_rs, na_ss, na_rs, nb_ss, nb_rs,
):
    i = lax.axis_index("row")
    j = lax.axis_index("col")
    x = j // NZ
    z = lax.rem(j, NZ)
    q = i // 2
    core = lax.rem(i, 2)
    twin = (q * 2 + 1 - core, j)

    def row_peer(d):
        return (turn(i, d, NG), j)

    def col_peer(d):
        return (i, turn(j, d, NG))

    def x_peer(d):
        return (i, turn(x, d, NX) * NZ + z)

    def z_peer(d):
        return (i, x * NZ + turn(z, d, NZ))

    def tile_copy(c):
        part = pl.ds(c * (K // 4), K // 4)
        return pltpu.make_async_copy(tiles.at[0, 0, part], t.at[part], t_sem.at[c])

    for c in range(4):
        tile_copy(c).start()

    for buf in (ca, cb, na, nb):
        buf[...] = jnp.zeros_like(buf)

    barrier = pltpu.get_barrier_semaphore()

    def greet(d):
        pl.semaphore_signal(barrier, inc=1, device_id=row_peer(d + 1), device_id_type=MESH)
        pl.semaphore_signal(barrier, inc=1, device_id=col_peer(d + 1), device_id_type=MESH)

    repeat(NG - 1, greet)

    def cut_dir(b):
        for r in range(RHS):
            dpiece[r, pl.ds(b, 1), :] = dirn[pl.ds(r, 1), pl.ds(pl.multiple_of(b * TB, TB), TB)]

    def cut_res(b):
        for r in range(RHS):
            rpiece[r, pl.ds(b, 1), :] = res[pl.ds(r, 1), pl.ds(pl.multiple_of(b * TB, TB), TB)]

    repeat(PC, cut_dir, unroll=4)
    xg[i] = dpiece[...].astype(BF16)
    repeat(PR, cut_res, unroll=4)
    rg[j] = rpiece[...].astype(BF16)

    pl.semaphore_wait(barrier, 2 * (NG - 1))

    def send_x(d):
        peer = (turn(q, d + 1, NQ) * 2 + core, j)
        return remote(xg.at[i], xg.at[i], x_ss.at[d], x_rs.at[d], peer)

    def take_x(d):
        s = turn(q, -d - 1, NQ) * 2 + core
        return remote(xg.at[s], xg.at[s], x_ss.at[d], x_rs.at[d], twin)

    def send_twin(d):
        s = turn(q, -d, NQ) * 2 + core
        return remote(xg.at[s], xg.at[s], t_ss.at[d], t_rs.at[d], twin)

    def take_twin(d):
        s = turn(q, -d, NQ) * 2 + 1 - core
        return remote(xg.at[s], xg.at[s], t_ss.at[d], t_rs.at[d], twin)

    def z_send(buf, ss, rs, d):
        return remote(buf.at[j], buf.at[j], ss.at[d], rs.at[d], z_peer(d + 1))

    def z_take(buf, ss, rs, d):
        s = x * NZ + turn(z, -d - 1, NZ)
        return remote(buf.at[s], buf.at[s], ss.at[d], rs.at[d], z_peer(d + 1))

    def x_send(buf, ss, rs, e, d):
        s = x * NZ + turn(z, -e, NZ)
        return remote(buf.at[s], buf.at[s], ss.at[e, d], rs.at[e, d], x_peer(d + 1))

    def x_take(buf, ss, rs, e, d):
        s = turn(x, -d - 1, NX) * NZ + turn(z, -e, NZ)
        return remote(buf.at[s], buf.at[s], ss.at[e, d], rs.at[e, d], x_peer(d + 1))

    def gather_first(buf, zs, zr, xs, xr):
        for d in FAR_FIRST:
            z_send(buf, zs, zr, d).start()
        for d in FAR_FIRST:
            x_send(buf, xs, xr, 0, d).start()

    def gather_forward(buf, zs, zr, xs, xr):
        for d in FAR_LAST:
            z_take(buf, zs, zr, d).wait_recv()
            for f in FAR_FIRST:
                x_send(buf, xs, xr, d + 1, f).start()

    def gather_sent(buf, zs, zr, xs, xr):
        repeat(NZ - 1, lambda d: z_send(buf, zs, zr, d).wait_send())
        repeat(NZ, lambda e: repeat(NX - 1, lambda d: x_send(buf, xs, xr, e, d).wait_send()))

    repeat(NQ - 1, lambda d: send_x(d).start())
    send_twin(0).start()
    old = (rg, rz_ss, rz_rs, rx_ss, rx_rs)
    new = (ag, az_ss, az_rs, ax_ss, ax_rs)
    gather_first(*old)

    idx[...] = jnp.zeros_like(idx)
    idx[0:1, 0:K] = rows_v[0]
    idx[1:2, 0:K] = cols_v[0]
    count = count_s[0, 0]
    used = lax.broadcasted_iota(jnp.int32, (TB, KPAD), 1) < count
    down = lax.broadcasted_iota(jnp.int32, (TB, KPAD), 0)
    for c in range(BR // TB):
        hit = jnp.where((down + c * TB == idx[0:1, :]) & used, 1.0, 0.0).astype(BF16)
        hit_r[c * TB : (c + 1) * TB, 0:KPAD] = hit
        hit_r[c * TB : (c + 1) * TB, KPAD : 2 * KPAD] = hit
    for c in range(BC // TB):
        hit = jnp.where((down + c * TB == idx[1:2, :]) & used, 1.0, 0.0).astype(BF16)
        hit_c[c * TB : (c + 1) * TB, 0:KPAD] = hit
        hit_c[c * TB : (c + 1) * TB, KPAD : 2 * KPAD] = hit
    hilo[K:KPAD, :] = jnp.zeros((KPAD - K, RHS * TB), BF16)
    hilo[KPAD + K :, :] = jnp.zeros((KPAD - K, RHS * TB), BF16)

    top = lax.broadcasted_iota(jnp.int32, (8, TB), 0) < RHS
    slot = lax.broadcasted_iota(jnp.int32, (HALF, TB), 0)

    def spread(src, dst, p, blocks):
        at = pl.ds(pl.multiple_of(p * blocks, blocks), blocks)
        for r in range(RHS):
            v = src[p, r].astype(F32)
            dst[at, r, :] = v
            dst[at, RHS + r, :] = v

    def products(vec, index_s, transpose):
        axis = 0 if transpose else 1

        def four(k):
            v = [vec[index_s[0, 0, k + n * QUARTER]] for n in range(4)]
            lhs = jnp.concatenate(
                [
                    jnp.concatenate([jnp.where(top, v[n], 0.0), jnp.where(top, 0.0, v[n + 2])], axis=1)
                    for n in range(2)
                ],
                axis=0,
            )
            rhs = jnp.concatenate(
                [
                    jnp.concatenate([t[k + n * QUARTER], t[k + n * QUARTER + HALF]], axis=axis)
                    for n in range(2)
                ],
                axis=1 - axis,
            )
            y = lax.dot_general(
                lhs.astype(BF16), rhs, (((1,), (axis,)), ((), ())), preferred_element_type=F32
            )
            ys[k] = y[0:8, 0:TB]
            ys[k + QUARTER] = y[8:16, TB : 2 * TB]

        repeat(QUARTER, four, unroll=40)
        for h in range(2):
            live = slot + h * HALF < count
            at = pl.ds(h * HALF, HALF)
            low_at = pl.ds(KPAD + h * HALF, HALF)
            for r in range(RHS):
                y = jnp.where(live, ys[:, h * RHS + r, :], 0.0)
                high = y.astype(BF16)
                hilo[at, r * TB : (r + 1) * TB] = high
                hilo[low_at, r * TB : (r + 1) * TB] = (y - high.astype(F32)).astype(BF16)

    def take_dir(d):
        take_x(d).wait_recv()
        send_twin(d + 1).start()
        spread(xg, xf, turn(q, -d - 1, NQ) * 2 + core, PC)

    def take_other(d):
        take_twin(d).wait_recv()
        spread(xg, xf, turn(q, -d, NQ) * 2 + 1 - core, PC)

    spread(xg, xf, i, PC)
    repeat(NQ - 1, take_dir)
    gather_forward(*old)
    repeat(NQ, take_other)
    for c in range(4):
        tile_copy(c).wait()
    products(xf, cols_s, False)

    def s1_send(d, e):
        p = turn(x, d + 1, NX) * NZ + turn(z, e + 1, NZ)
        dst = r1.at[turn(z, e + 1, NZ), x]
        return remote(sb.at[p], dst, s1_ss.at[d, e], s1_rs.at[d, e], x_peer(d + 1))

    def s1_take(d, e):
        dst = r1.at[turn(z, e + 1, NZ), turn(x, -d - 1, NX)]
        return remote(dst, dst, s1_ss.at[d, e], s1_rs.at[d, e], x_peer(d + 1))

    def s2_send(e):
        return remote(
            sb.at[x * NZ + turn(z, e + 1, NZ)], r2.at[z], s2_ss.at[e], s2_rs.at[e], z_peer(e + 1)
        )

    def s2_take(e):
        dst = r2.at[turn(z, -e - 1, NZ)]
        return remote(dst, dst, s2_ss.at[e], s2_rs.at[e], z_peer(e + 1))

    def image_chunk(d):
        xd = turn(x, d + 1, NX)
        hit = hit_r[pl.ds(pl.multiple_of(xd * TB, TB), TB), :]
        part = lax.dot_general(hit, hilo[...], (((1,), (0,)), ((), ())), preferred_element_type=F32)
        for q in range(NZ):
            for r in range(RHS):
                sb[xd * NZ + q, r] = part[q * PR : (q + 1) * PR, r * TB : (r + 1) * TB].astype(BF16)

    repeat(NX - 1, image_chunk)
    for e in FAR_FIRST + (NZ - 1,):
        for d in FAR_FIRST:
            s1_send(d, e).start()
    image_chunk(NX - 1)

    spread(rg, rf, j, PR)

    def take_res(e):
        def one(d):
            x_take(*((rg,) + old[3:]), e, d).wait_recv()
            spread(rg, rf, turn(x, -d - 1, NX) * NZ + turn(z, -e, NZ), PR)

        repeat(NX - 1, one)

    repeat(NZ, take_res)
    repeat(NZ - 1, lambda d: spread(rg, rf, x * NZ + turn(z, -d - 1, NZ), PR))
    products(rf, rows_s, True)
    for c in range(BC // TB):
        grad_r[c * TB : (c + 1) * TB, :] = lax.dot_general(
            hit_c[c * TB : (c + 1) * TB, :], hilo[...], (((1,), (0,)), ((), ())),
            preferred_element_type=F32,
        )

    def over_x(e):
        zt = turn(z, e + 1, NZ)
        repeat(NX - 1, lambda d: s1_take(d, e).wait_recv())
        total = sb[x * NZ + zt].astype(F32)
        for d in range(NX - 1):
            total += r1[zt, turn(x, -d - 1, NX)].astype(F32)
        return total

    def through(e):
        sb[x * NZ + turn(z, e + 1, NZ)] = over_x(e).astype(BF16)
        s2_send(e).start()

    for e in FAR_FIRST:
        through(e)
    image[...] = over_x(NZ - 1)

    def add_image(e):
        s2_take(e).wait_recv()
        image[...] += r2[turn(z, -e - 1, NZ)].astype(F32)

    for e in FAR_LAST:
        add_image(e)

    ag[j] = image[...].astype(BF16)
    gather_first(*new)

    def share(buf, me, peer, ss, rs):
        return lambda d: remote(buf.at[me], buf.at[me], ss.at[d], rs.at[d], peer(d + 1))

    def shared(buf, me, peer, ss, rs):
        def take(d):
            s = turn(me, -d - 1, NG)
            remote(buf.at[s], buf.at[s], ss.at[d], rs.at[d], peer(d + 1)).wait_recv()

        repeat(NG - 1, take)
        return jnp.sum(buf[...], axis=0)

    for r in range(RHS):
        v = image[r]
        ca[j, r : r + 1, :] = jnp.sum(v * v, axis=0, keepdims=True)
    c_col = (ca, j, col_peer, ca_ss, ca_rs)
    c_row = (cb, i, row_peer, cb_ss, cb_rs)
    repeat(NG - 1, lambda d: share(*c_col)(d).start())
    gather_forward(*new)
    cb[i] = shared(*c_col)
    repeat(NG - 1, lambda d: share(*c_row)(d).start())

    def write_image(b):
        for r in range(RHS):
            at = pl.ds(pl.multiple_of(b * TB, TB), TB)
            out_image[pl.ds(r, 1), at] = image[r, pl.ds(b, 1), :]

    repeat(PR, write_image, unroll=4)
    line = lax.broadcasted_iota(jnp.int32, (RHS, 1), 0)
    gamma = jnp.full((RHS, 1), gamma_s[0], F32)
    for r in range(1, RHS):
        gamma = jnp.where(line == r, gamma_s[r], gamma)

    spread(ag, rf, j, PR)
    repeat(NZ - 1, lambda d: spread(ag, rf, x * NZ + turn(z, -d - 1, NZ), PR))

    def take_image(e):
        def one(d):
            x_take(*((ag,) + new[3:]), e, d).wait_recv()
            spread(ag, rf, turn(x, -d - 1, NX) * NZ + turn(z, -e, NZ), PR)

        repeat(NX - 1, one)

    for e in (0, 1, 3, 2):
        take_image(e)
    products(rf, rows_s, True)

    def g_send(d):
        return remote(gs.at[turn(i, d + 1, NG)], gr.at[i], g_ss.at[d], g_rs.at[d], row_peer(d + 1))

    def g_take(d):
        dst = gr.at[turn(i, -d - 1, NG)]
        return remote(dst, dst, g_ss.at[d], g_rs.at[d], row_peer(d + 1))

    curvature = jnp.sum(shared(*c_row)[0:RHS, :], axis=1, keepdims=True)
    step = gamma / curvature
    out_scale[0] = jnp.broadcast_to(step, (RHS, TB))
    step_wide = jnp.concatenate(
        [jnp.broadcast_to(step[r : r + 1, :], (1, TB)) for r in range(RHS)], axis=1
    )
    for c in range(BC // TB):
        part = lax.dot_general(
            hit_c[c * TB : (c + 1) * TB, :], hilo[...], (((1,), (0,)), ((), ())),
            preferred_element_type=F32,
        )
        part = grad_r[c * TB : (c + 1) * TB, :] - step_wide * part
        for q in range(TB // PC):
            for r in range(RHS):
                gs[c * (TB // PC) + q, r] = part[
                    q * PC : (q + 1) * PC, r * TB : (r + 1) * TB
                ].astype(BF16)
    repeat(NG - 1, lambda d: g_send(d).start())

    repeat(NQ - 1, lambda d: send_x(d).wait_send())
    repeat(NQ, lambda d: send_twin(d).wait_send())
    gather_sent(*old)
    gather_sent(*new)
    repeat(NX - 1, lambda d: repeat(NZ, lambda e: s1_send(d, e).wait_send()))
    repeat(NZ - 1, lambda e: s2_send(e).wait_send())
    repeat(NG - 1, lambda d: share(*c_col)(d).wait_send())
    repeat(NG - 1, lambda d: share(*c_row)(d).wait_send())

    repeat(NG - 1, lambda d: g_take(d).wait_recv())
    gr[i] = gs[i]
    grad = gr[0].astype(F32)
    for s in range(1, NG):
        grad += gr[s].astype(F32)

    for r in range(RHS):
        v = grad[r]
        na[i, r : r + 1, :] = jnp.sum(v * v, axis=0, keepdims=True)
    n_row = (na, i, row_peer, na_ss, na_rs)
    n_col = (nb, j, col_peer, nb_ss, nb_rs)
    repeat(NG - 1, lambda d: share(*n_row)(d).start())
    for r in range(RHS):
        for b in range(PC):
            out_grad[r : r + 1, b * TB : (b + 1) * TB] = grad[r, b : b + 1, :]
    nb[j] = shared(*n_row)
    repeat(NG - 1, lambda d: share(*n_col)(d).start())
    norm_next = jnp.sum(shared(*n_col)[0:RHS, :], axis=1, keepdims=True)
    out_scale[1] = jnp.broadcast_to(norm_next / gamma, (RHS, TB))

    repeat(NG - 1, lambda d: g_send(d).wait_send())
    repeat(NG - 1, lambda d: share(*n_row)(d).wait_send())
    repeat(NG - 1, lambda d: share(*n_col)(d).wait_send())


def finish(sol, res, dirn, image, gradient, scale, out_sol, out_res, out_dir):
    step = scale[0, :, 0:1]
    beta = scale[1, :, 0:1]
    out_sol[...] = sol[...] + step * dirn[...]
    out_res[...] = res[...] - step * image[...]
    out_dir[...] = gradient[...] + beta * dirn[...]


def on_device(
    tile_values, tile_rows, tile_cols, tile_counts, solution, residual, direction, grad_norm
):
    smem = pl.BlockSpec(memory_space=pltpu.SMEM)
    vmem = pl.BlockSpec(memory_space=pltpu.VMEM)
    piece_r = (RHS, PR, TB)
    piece_c = (RHS, PC, TB)
    dma = pltpu.SemaphoreType.DMA
    peers = [dma((NG - 1,)), dma((NG - 1,))]
    staged = [dma((NZ - 1,)), dma((NZ - 1,)), dma((NZ, NX - 1)), dma((NZ, NX - 1))]
    image, gradient, scale = pl.pallas_call(
        kernel,
        out_shape=(
            jax.ShapeDtypeStruct(residual.shape, F32),
            jax.ShapeDtypeStruct(direction.shape, F32),
            jax.ShapeDtypeStruct((2, RHS, TB), F32),
        ),
        in_specs=[smem, smem, smem, smem, vmem, vmem, pl.BlockSpec(memory_space=pltpu.HBM)]
        + [vmem] * 2,
        out_specs=(vmem, vmem, vmem),
        scratch_shapes=[
            pltpu.VMEM((K, TB, TB), BF16),
            pltpu.VMEM((NG,) + piece_c, BF16),
            pltpu.VMEM((NG,) + piece_r, BF16),
            pltpu.VMEM((NG,) + piece_r, BF16),
            pltpu.VMEM((NG,) + piece_r, BF16),
            pltpu.VMEM((NZ, NX) + piece_r, BF16),
            pltpu.VMEM((NZ,) + piece_r, BF16),
            pltpu.VMEM((NG,) + piece_c, BF16),
            pltpu.VMEM((NG,) + piece_c, BF16),
            pltpu.VMEM(piece_c, F32),
            pltpu.VMEM(piece_r, F32),
            pltpu.VMEM(piece_r, F32),
            pltpu.VMEM((BC, 2 * RHS, TB), F32),
            pltpu.VMEM((BR, 2 * RHS, TB), F32),
            pltpu.VMEM((HALF, 2 * RHS, TB), F32),
            pltpu.VMEM((2 * KPAD, RHS * TB), BF16),
            pltpu.VMEM((BR, 2 * KPAD), BF16),
            pltpu.VMEM((BC, 2 * KPAD), BF16),
            pltpu.VMEM((BC, RHS * TB), F32),
            pltpu.VMEM((8, KPAD), jnp.int32),
            pltpu.VMEM((NG, 8, TB), F32),
            pltpu.VMEM((NG, 8, TB), F32),
            pltpu.VMEM((NG, 8, TB), F32),
            pltpu.VMEM((NG, 8, TB), F32),
            dma((4,)),
            dma((NQ - 1,)), dma((NQ - 1,)),
            dma((NQ,)), dma((NQ,)),
            *staged,
            dma((NX - 1, NZ)), dma((NX - 1, NZ)),
            dma((NZ - 1,)), dma((NZ - 1,)),
            *staged,
            *peers,
            *peers, *peers, *peers, *peers,
        ],
        compiler_params=pltpu.CompilerParams(
            collective_id=0, has_side_effects=True, vmem_limit_bytes=60 * 1024 * 1024
        ),
    )(
        tile_counts, tile_rows, tile_cols, grad_norm, tile_rows, tile_cols,
        tile_values, residual, direction,
    )
    return pl.pallas_call(
        finish,
        out_shape=tuple(
            jax.ShapeDtypeStruct(a.shape, F32) for a in (solution, residual, direction)
        ),
        in_specs=[vmem] * 6,
        out_specs=(vmem, vmem, vmem),
    )(solution, residual, direction, image, gradient, scale)


def solution(mesh):
    in_specs = (
        P("row", "col", None, None, None),
        P("row", "col", None),
        P("row", "col", None),
        P("row", "col"),
        P(None, ("col", "row")),
        P(None, ("row", "col")),
        P(None, ("col", "row")),
        P(),
    )
    out_specs = (P(None, ("col", "row")), P(None, ("row", "col")), P(None, ("col", "row")))
    return jax.shard_map(
        on_device, mesh=mesh, in_specs=in_specs, out_specs=out_specs, check_vma=False
    )
```

```python
import jax
import jax.numpy as jnp
from jax import lax
from jax.experimental import pallas as pl
from jax.experimental.pallas import tpu as pltpu
from jax.sharding import PartitionSpec as P

TB = 128
RHS = 4
BR = 512
BC = 256
K = 320
HALF = K // 2
QUARTER = K // 4
KPAD = 384
NG = 16
NX = 4
NZ = 4
FAR_FIRST = (1, 0, 2)
FAR_LAST = (0, 2, 1)
NQ = NG // 2
PR = BR // NG
PC = BC // NG
F32 = jnp.float32
BF16 = jnp.bfloat16
MESH = pl.DeviceIdType.MESH


def remote(src, dst, send_sem, recv_sem, device):
    return pltpu.make_async_remote_copy(
        src_ref=src,
        dst_ref=dst,
        send_sem=send_sem,
        recv_sem=recv_sem,
        device_id=device,
        device_id_type=MESH,
    )


def turn(base, step, size):
    return lax.rem(base + step + size, size)


def repeat(count, body, unroll=1):
    def step(index, carry):
        body(index)
        return carry

    lax.fori_loop(0, count, step, 0, unroll=unroll)


def kernel(
    count_s, rows_s, cols_s, gamma_s, rows_v, cols_v, tiles, res, dirn,
    out_image, out_grad, out_scale,
    t, xg, ag, rg, sb, r1, r2, gs, gr, hs, hr, dpiece, rpiece, image, xf, rf, ys, hilo, hit_r, hit_c,
    grad_r, idx, ca, cb, na, nb,
    met, t_sem, x_ss, x_rs, t_ss, t_rs, rz_ss, rz_rs, rx_ss, rx_rs, s1_ss, s1_rs, s2_ss, s2_rs,
    az_ss, az_rs, ax_ss, ax_rs, g_ss, g_rs, h_ss, h_rs, ca_ss, ca_rs, cb_ss, cb_rs, na_ss, na_rs, nb_ss, nb_rs,
):
    i = lax.axis_index("row")
    j = lax.axis_index("col")
    x = j // NZ
    z = lax.rem(j, NZ)
    q = i // 2
    core = lax.rem(i, 2)
    twin = (q * 2 + 1 - core, j)

    def row_peer(d):
        return (turn(i, d, NG), j)

    def col_peer(d):
        return (i, turn(j, d, NG))

    def x_peer(d):
        return (i, turn(x, d, NX) * NZ + z)

    def z_peer(d):
        return (i, x * NZ + turn(z, d, NZ))

    def tile_copy(c):
        part = pl.ds(c * (K // 4), K // 4)
        return pltpu.make_async_copy(tiles.at[0, 0, part], t.at[part], t_sem.at[c])

    for c in range(4):
        tile_copy(c).start()

    for buf in (ca, cb, na, nb):
        buf[...] = jnp.zeros_like(buf)

    barrier = pltpu.get_barrier_semaphore()

    def greet(device):
        pl.semaphore_signal(barrier, inc=1, device_id=device, device_id_type=MESH)

    repeat(NG - 1, lambda d: greet(row_peer(d + 1)))
    for d in FAR_FIRST:
        greet(x_peer(d + 1))
    for d in (0, 2):
        greet(z_peer(d + 1))

    def cut_dir(b):
        for r in range(RHS):
            dpiece[r, pl.ds(b, 1), :] = dirn[pl.ds(r, 1), pl.ds(pl.multiple_of(b * TB, TB), TB)]

    def cut_res(b):
        for r in range(RHS):
            rpiece[r, pl.ds(b, 1), :] = res[pl.ds(r, 1), pl.ds(pl.multiple_of(b * TB, TB), TB)]

    repeat(PC, cut_dir, unroll=4)
    xg[i] = dpiece[...].astype(BF16)
    repeat(PR, cut_res, unroll=4)
    rg[j] = rpiece[...].astype(BF16)

    pl.semaphore_wait(barrier, NG - 1 + NX - 1 + 2)
    pl.semaphore_signal(met, inc=1, device_id=z_peer(1), device_id_type=MESH)

    def send_x(d):
        peer = (turn(q, d + 1, NQ) * 2 + core, j)
        return remote(xg.at[i], xg.at[i], x_ss.at[d], x_rs.at[d], peer)

    def take_x(d):
        s = turn(q, -d - 1, NQ) * 2 + core
        return remote(xg.at[s], xg.at[s], x_ss.at[d], x_rs.at[d], twin)

    def send_twin(d):
        s = turn(q, -d, NQ) * 2 + core
        return remote(xg.at[s], xg.at[s], t_ss.at[d], t_rs.at[d], twin)

    def take_twin(d):
        s = turn(q, -d, NQ) * 2 + 1 - core
        return remote(xg.at[s], xg.at[s], t_ss.at[d], t_rs.at[d], twin)

    def z_send(buf, ss, rs, d):
        return remote(buf.at[j], buf.at[j], ss.at[d], rs.at[d], z_peer(d + 1))

    def z_take(buf, ss, rs, d):
        s = x * NZ + turn(z, -d - 1, NZ)
        return remote(buf.at[s], buf.at[s], ss.at[d], rs.at[d], z_peer(d + 1))

    def x_send(buf, ss, rs, e, d):
        s = x * NZ + turn(z, -e, NZ)
        return remote(buf.at[s], buf.at[s], ss.at[e, d], rs.at[e, d], x_peer(d + 1))

    def x_take(buf, ss, rs, e, d):
        s = turn(x, -d - 1, NX) * NZ + turn(z, -e, NZ)
        return remote(buf.at[s], buf.at[s], ss.at[e, d], rs.at[e, d], x_peer(d + 1))

    def gather_first(buf, zs, zr, xs, xr):
        for d in FAR_FIRST:
            z_send(buf, zs, zr, d).start()
        for d in FAR_FIRST:
            x_send(buf, xs, xr, 0, d).start()

    def gather_forward(buf, zs, zr, xs, xr):
        for d in FAR_LAST:
            z_take(buf, zs, zr, d).wait_recv()
            for f in FAR_FIRST:
                x_send(buf, xs, xr, d + 1, f).start()

    def gather_sent(buf, zs, zr, xs, xr):
        repeat(NZ - 1, lambda d: z_send(buf, zs, zr, d).wait_send())
        repeat(NZ, lambda e: repeat(NX - 1, lambda d: x_send(buf, xs, xr, e, d).wait_send()))

    repeat(NQ - 1, lambda d: send_x(d).start())
    send_twin(0).start()
    old = (rg, rz_ss, rz_rs, rx_ss, rx_rs)
    new = (ag, az_ss, az_rs, ax_ss, ax_rs)
    pl.semaphore_wait(met, 1)
    gather_first(*old)

    idx[...] = jnp.zeros_like(idx)
    idx[0:1, 0:K] = rows_v[0]
    idx[1:2, 0:K] = cols_v[0]
    count = count_s[0, 0]
    used = lax.broadcasted_iota(jnp.int32, (TB, KPAD), 1) < count
    down = lax.broadcasted_iota(jnp.int32, (TB, KPAD), 0)
    for c in range(BR // TB):
        hit = jnp.where((down + c * TB == idx[0:1, :]) & used, 1.0, 0.0).astype(BF16)
        hit_r[c * TB : (c + 1) * TB, 0:KPAD] = hit
        hit_r[c * TB : (c + 1) * TB, KPAD : 2 * KPAD] = hit
    for c in range(BC // TB):
        hit = jnp.where((down + c * TB == idx[1:2, :]) & used, 1.0, 0.0).astype(BF16)
        hit_c[c * TB : (c + 1) * TB, 0:KPAD] = hit
        hit_c[c * TB : (c + 1) * TB, KPAD : 2 * KPAD] = hit
    hilo[K:KPAD, :] = jnp.zeros((KPAD - K, RHS * TB), BF16)
    hilo[KPAD + K :, :] = jnp.zeros((KPAD - K, RHS * TB), BF16)

    top = lax.broadcasted_iota(jnp.int32, (8, TB), 0) < RHS
    slot = lax.broadcasted_iota(jnp.int32, (HALF, TB), 0)

    def spread(src, dst, p, blocks):
        at = pl.ds(pl.multiple_of(p * blocks, blocks), blocks)
        for r in range(RHS):
            v = src[p, r].astype(F32)
            dst[at, r, :] = v
            dst[at, RHS + r, :] = v

    def products(vec, index_s, transpose, between=None):
        axis = 0 if transpose else 1

        def four(k):
            v = [vec[index_s[0, 0, k + n * QUARTER]] for n in range(4)]
            lhs = jnp.concatenate(
                [
                    jnp.concatenate([jnp.where(top, v[n], 0.0), jnp.where(top, 0.0, v[n + 2])], axis=1)
                    for n in range(2)
                ],
                axis=0,
            )
            rhs = jnp.concatenate(
                [
                    jnp.concatenate([t[k + n * QUARTER], t[k + n * QUARTER + HALF]], axis=axis)
                    for n in range(2)
                ],
                axis=1 - axis,
            )
            y = lax.dot_general(
                lhs.astype(BF16), rhs, (((1,), (axis,)), ((), ())), preferred_element_type=F32
            )
            ys[k] = y[0:8, 0:TB]
            ys[k + QUARTER] = y[8:16, TB : 2 * TB]

        half = QUARTER // 2
        repeat(half, four, unroll=half)
        if between is not None:
            between()
        repeat(half, lambda k: four(k + half), unroll=half)
        for h in range(2):
            live = slot + h * HALF < count
            at = pl.ds(h * HALF, HALF)
            low_at = pl.ds(KPAD + h * HALF, HALF)
            for r in range(RHS):
                y = jnp.where(live, ys[:, h * RHS + r, :], 0.0)
                high = y.astype(BF16)
                hilo[at, r * TB : (r + 1) * TB] = high
                hilo[low_at, r * TB : (r + 1) * TB] = (y - high.astype(F32)).astype(BF16)

    def grad_chunk(buf, c):
        part = lax.dot_general(
            hit_c[c * TB : (c + 1) * TB, :], hilo[...], (((1,), (0,)), ((), ())),
            preferred_element_type=F32,
        )
        for n in range(TB // PC):
            for r in range(RHS):
                buf[c * (TB // PC) + n, r] = part[
                    n * PC : (n + 1) * PC, r * TB : (r + 1) * TB
                ].astype(BF16)

    def g_send(src, dst, ss, rs, d):
        return remote(src.at[turn(i, d + 1, NG)], dst.at[i], ss.at[d], rs.at[d], row_peer(d + 1))

    def g_sum(src, dst, ss, rs):
        def take(d):
            slot = dst.at[turn(i, -d - 1, NG)]
            remote(slot, slot, ss.at[d], rs.at[d], row_peer(d + 1)).wait_recv()

        repeat(NG - 1, take)
        dst[i] = src[i]
        total = dst[0].astype(F32)
        for n in range(1, NG):
            total += dst[n].astype(F32)
        return total

    g_old = (hs, hr, h_ss, h_rs)
    g_new = (gs, gr, g_ss, g_rs)

    def take_dir(d):
        take_x(d).wait_recv()
        send_twin(d + 1).start()
        spread(xg, xf, turn(q, -d - 1, NQ) * 2 + core, PC)

    def take_other(d):
        take_twin(d).wait_recv()
        spread(xg, xf, turn(q, -d, NQ) * 2 + 1 - core, PC)

    spread(xg, xf, i, PC)
    repeat(NQ - 1, take_dir)
    gather_forward(*old)
    repeat(NQ, take_other)
    for c in range(4):
        tile_copy(c).wait()
    products(xf, cols_s, False)

    def s1_send(d, e):
        p = turn(x, d + 1, NX) * NZ + turn(z, e + 1, NZ)
        dst = r1.at[turn(z, e + 1, NZ), x]
        return remote(sb.at[p], dst, s1_ss.at[d, e], s1_rs.at[d, e], x_peer(d + 1))

    def s1_take(d, e):
        dst = r1.at[turn(z, e + 1, NZ), turn(x, -d - 1, NX)]
        return remote(dst, dst, s1_ss.at[d, e], s1_rs.at[d, e], x_peer(d + 1))

    def s2_send(e):
        return remote(
            sb.at[x * NZ + turn(z, e + 1, NZ)], r2.at[z], s2_ss.at[e], s2_rs.at[e], z_peer(e + 1)
        )

    def s2_take(e):
        dst = r2.at[turn(z, -e - 1, NZ)]
        return remote(dst, dst, s2_ss.at[e], s2_rs.at[e], z_peer(e + 1))

    def image_chunk(d):
        xd = turn(x, d + 1, NX)
        hit = hit_r[pl.ds(pl.multiple_of(xd * TB, TB), TB), :]
        part = lax.dot_general(hit, hilo[...], (((1,), (0,)), ((), ())), preferred_element_type=F32)
        for q in range(NZ):
            for r in range(RHS):
                sb[xd * NZ + q, r] = part[q * PR : (q + 1) * PR, r * TB : (r + 1) * TB].astype(BF16)

    repeat(NX - 1, image_chunk)
    for e in FAR_FIRST + (NZ - 1,):
        for d in FAR_FIRST:
            s1_send(d, e).start()
    image_chunk(NX - 1)

    def over_x(e):
        zt = turn(z, e + 1, NZ)
        repeat(NX - 1, lambda d: s1_take(d, e).wait_recv())
        total = sb[x * NZ + zt].astype(F32)
        for d in range(NX - 1):
            total += r1[zt, turn(x, -d - 1, NX)].astype(F32)
        return total

    def through(e):
        sb[x * NZ + turn(z, e + 1, NZ)] = over_x(e).astype(BF16)
        s2_send(e).start()

    for e in FAR_FIRST:
        through(e)
    image[...] = over_x(NZ - 1)

    spread(rg, rf, j, PR)

    def take_res(e):
        def one(d):
            x_take(*((rg,) + old[3:]), e, d).wait_recv()
            spread(rg, rf, turn(x, -d - 1, NX) * NZ + turn(z, -e, NZ), PR)

        repeat(NX - 1, one)

    repeat(NZ, take_res)
    repeat(NZ - 1, lambda d: spread(rg, rf, x * NZ + turn(z, -d - 1, NZ), PR))
    products(rf, rows_s, True)
    for c in range(BC // TB):
        grad_chunk(hs, c)

    def add_image(e):
        s2_take(e).wait_recv()
        image[...] += r2[turn(z, -e - 1, NZ)].astype(F32)

    for e in FAR_LAST:
        add_image(e)

    ag[j] = image[...].astype(BF16)
    gather_first(*new)

    def share(buf, me, peer, ss, rs):
        return lambda d: remote(buf.at[me], buf.at[me], ss.at[d], rs.at[d], peer(d + 1))

    def shared(buf, me, peer, ss, rs):
        def take(d):
            s = turn(me, -d - 1, NG)
            remote(buf.at[s], buf.at[s], ss.at[d], rs.at[d], peer(d + 1)).wait_recv()

        repeat(NG - 1, take)
        return jnp.sum(buf[...], axis=0)

    for r in range(RHS):
        v = image[r]
        ca[j, r : r + 1, :] = jnp.sum(v * v, axis=0, keepdims=True)
    c_col = (ca, j, col_peer, ca_ss, ca_rs)
    c_row = (cb, i, row_peer, cb_ss, cb_rs)
    repeat(NG - 1, lambda d: share(*c_col)(d).start())
    gather_forward(*new)
    repeat(NG - 1, lambda d: g_send(*g_old, d).start())
    cb[i] = shared(*c_col)
    repeat(NG - 1, lambda d: share(*c_row)(d).start())

    def write_image(b):
        for r in range(RHS):
            at = pl.ds(pl.multiple_of(b * TB, TB), TB)
            out_image[pl.ds(r, 1), at] = image[r, pl.ds(b, 1), :]

    repeat(PR, write_image, unroll=4)
    line = lax.broadcasted_iota(jnp.int32, (RHS, 1), 0)
    gamma = jnp.full((RHS, 1), gamma_s[0], F32)
    for r in range(1, RHS):
        gamma = jnp.where(line == r, gamma_s[r], gamma)

    spread(ag, rf, j, PR)
    repeat(NZ - 1, lambda d: spread(ag, rf, x * NZ + turn(z, -d - 1, NZ), PR))

    def take_image(e):
        def one(d):
            x_take(*((ag,) + new[3:]), e, d).wait_recv()
            spread(ag, rf, turn(x, -d - 1, NX) * NZ + turn(z, -e, NZ), PR)

        repeat(NX - 1, one)

    for e in (0, 1, 3, 2):
        take_image(e)
    products(rf, rows_s, True)

    for c in range(BC // TB):
        grad_chunk(gs, c)
    repeat(NG - 1, lambda d: g_send(*g_new, d).start())

    repeat(NQ - 1, lambda d: send_x(d).wait_send())
    repeat(NQ, lambda d: send_twin(d).wait_send())
    gather_sent(*old)
    gather_sent(*new)
    repeat(NX - 1, lambda d: repeat(NZ, lambda e: s1_send(d, e).wait_send()))
    repeat(NZ - 1, lambda e: s2_send(e).wait_send())
    repeat(NG - 1, lambda d: share(*c_col)(d).wait_send())
    repeat(NG - 1, lambda d: share(*c_row)(d).wait_send())

    grad_r[...] = g_sum(*g_old)
    curvature = jnp.sum(shared(*c_row)[0:RHS, :], axis=1, keepdims=True)
    step = gamma / curvature
    out_scale[0] = jnp.broadcast_to(step, (RHS, TB))
    total = g_sum(*g_new)
    grad = [grad_r[r] - step[r : r + 1, :] * total[r] for r in range(RHS)]

    for r in range(RHS):
        v = grad[r]
        na[i, r : r + 1, :] = jnp.sum(v * v, axis=0, keepdims=True)
    n_row = (na, i, row_peer, na_ss, na_rs)
    n_col = (nb, j, col_peer, nb_ss, nb_rs)
    repeat(NG - 1, lambda d: share(*n_row)(d).start())
    for r in range(RHS):
        for b in range(PC):
            out_grad[r : r + 1, b * TB : (b + 1) * TB] = grad[r][b : b + 1, :]
    nb[j] = shared(*n_row)
    repeat(NG - 1, lambda d: share(*n_col)(d).start())
    norm_next = jnp.sum(shared(*n_col)[0:RHS, :], axis=1, keepdims=True)
    out_scale[1] = jnp.broadcast_to(norm_next / gamma, (RHS, TB))

    repeat(NG - 1, lambda d: g_send(*g_old, d).wait_send())
    repeat(NG - 1, lambda d: g_send(*g_new, d).wait_send())
    repeat(NG - 1, lambda d: share(*n_row)(d).wait_send())
    repeat(NG - 1, lambda d: share(*n_col)(d).wait_send())


def finish(sol, res, dirn, image, gradient, scale, out_sol, out_res, out_dir):
    step = scale[0, :, 0:1]
    beta = scale[1, :, 0:1]
    out_sol[...] = sol[...] + step * dirn[...]
    out_res[...] = res[...] - step * image[...]
    out_dir[...] = gradient[...] + beta * dirn[...]


def on_device(
    tile_values, tile_rows, tile_cols, tile_counts, solution, residual, direction, grad_norm
):
    smem = pl.BlockSpec(memory_space=pltpu.SMEM)
    vmem = pl.BlockSpec(memory_space=pltpu.VMEM)
    piece_r = (RHS, PR, TB)
    piece_c = (RHS, PC, TB)
    dma = pltpu.SemaphoreType.DMA
    peers = [dma((NG - 1,)), dma((NG - 1,))]
    staged = [dma((NZ - 1,)), dma((NZ - 1,)), dma((NZ, NX - 1)), dma((NZ, NX - 1))]
    image, gradient, scale = pl.pallas_call(
        kernel,
        out_shape=(
            jax.ShapeDtypeStruct(residual.shape, F32),
            jax.ShapeDtypeStruct(direction.shape, F32),
            jax.ShapeDtypeStruct((2, RHS, TB), F32),
        ),
        in_specs=[smem, smem, smem, smem, vmem, vmem, pl.BlockSpec(memory_space=pltpu.HBM)]
        + [vmem] * 2,
        out_specs=(vmem, vmem, vmem),
        scratch_shapes=[
            pltpu.VMEM((K, TB, TB), BF16),
            pltpu.VMEM((NG,) + piece_c, BF16),
            pltpu.VMEM((NG,) + piece_r, BF16),
            pltpu.VMEM((NG,) + piece_r, BF16),
            pltpu.VMEM((NG,) + piece_r, BF16),
            pltpu.VMEM((NZ, NX) + piece_r, BF16),
            pltpu.VMEM((NZ,) + piece_r, BF16),
            pltpu.VMEM((NG,) + piece_c, BF16),
            pltpu.VMEM((NG,) + piece_c, BF16),
            pltpu.VMEM((NG,) + piece_c, BF16),
            pltpu.VMEM((NG,) + piece_c, BF16),
            pltpu.VMEM(piece_c, F32),
            pltpu.VMEM(piece_r, F32),
            pltpu.VMEM(piece_r, F32),
            pltpu.VMEM((BC, 2 * RHS, TB), F32),
            pltpu.VMEM((BR, 2 * RHS, TB), F32),
            pltpu.VMEM((HALF, 2 * RHS, TB), F32),
            pltpu.VMEM((2 * KPAD, RHS * TB), BF16),
            pltpu.VMEM((BR, 2 * KPAD), BF16),
            pltpu.VMEM((BC, 2 * KPAD), BF16),
            pltpu.VMEM(piece_c, F32),
            pltpu.VMEM((8, KPAD), jnp.int32),
            pltpu.VMEM((NG, 8, TB), F32),
            pltpu.VMEM((NG, 8, TB), F32),
            pltpu.VMEM((NG, 8, TB), F32),
            pltpu.VMEM((NG, 8, TB), F32),
            pltpu.SemaphoreType.REGULAR,
            dma((4,)),
            dma((NQ - 1,)), dma((NQ - 1,)),
            dma((NQ,)), dma((NQ,)),
            *staged,
            dma((NX - 1, NZ)), dma((NX - 1, NZ)),
            dma((NZ - 1,)), dma((NZ - 1,)),
            *staged,
            *peers,
            *peers,
            *peers, *peers, *peers, *peers,
        ],
        compiler_params=pltpu.CompilerParams(
            collective_id=0, has_side_effects=True, vmem_limit_bytes=60 * 1024 * 1024
        ),
    )(
        tile_counts, tile_rows, tile_cols, grad_norm, tile_rows, tile_cols,
        tile_values, residual, direction,
    )
    return pl.pallas_call(
        finish,
        out_shape=tuple(
            jax.ShapeDtypeStruct(a.shape, F32) for a in (solution, residual, direction)
        ),
        in_specs=[vmem] * 6,
        out_specs=(vmem, vmem, vmem),
    )(solution, residual, direction, image, gradient, scale)


def solution(mesh):
    in_specs = (
        P("row", "col", None, None, None),
        P("row", "col", None),
        P("row", "col", None),
        P("row", "col"),
        P(None, ("col", "row")),
        P(None, ("row", "col")),
        P(None, ("col", "row")),
        P(),
    )
    out_specs = (P(None, ("col", "row")), P(None, ("row", "col")), P(None, ("col", "row")))
    return jax.shard_map(
        on_device, mesh=mesh, in_specs=in_specs, out_specs=out_specs, check_vma=False
    )
```

```python
import jax
import jax.numpy as jnp
from jax import lax
from jax.experimental import pallas as pl
from jax.experimental.pallas import tpu as pltpu
from jax.sharding import PartitionSpec as P

TB = 128
RHS = 4
BR = 512
BC = 256
K = 320
HALF = K // 2
QUARTER = K // 4
KPAD = 384
NG = 16
NX = 4
NZ = 4
FAR_FIRST = (1, 0, 2)
FAR_LAST = (0, 2, 1)
NQ = NG // 2
PR = BR // NG
PC = BC // NG
F32 = jnp.float32
BF16 = jnp.bfloat16
MESH = pl.DeviceIdType.MESH


def remote(src, dst, send_sem, recv_sem, device):
    return pltpu.make_async_remote_copy(
        src_ref=src,
        dst_ref=dst,
        send_sem=send_sem,
        recv_sem=recv_sem,
        device_id=device,
        device_id_type=MESH,
    )


def turn(base, step, size):
    return lax.rem(base + step + size, size)


def repeat(count, body, unroll=16):
    def step(index, carry):
        body(index)
        return carry

    lax.fori_loop(0, count, step, 0, unroll=min(unroll, count))


def kernel(
    count_s, rows_s, cols_s, gamma_s, rows_v, cols_v, tiles, res, dirn,
    out_image, out_grad, out_scale,
    t, xg, ag, rg, sb, r1, r2, gs, gr, hs, hr, dpiece, rpiece, image, xf, rf, ys, hilo, hit_r, hit_c,
    grad_r, idx, ca, cb, na, nb,
    met, t_sem, x_ss, x_rs, t_ss, t_rs, rz_ss, rz_rs, rx_ss, rx_rs, s1_ss, s1_rs, s2_ss, s2_rs,
    az_ss, az_rs, ax_ss, ax_rs, g_ss, g_rs, h_ss, h_rs, ca_ss, ca_rs, cb_ss, cb_rs, na_ss, na_rs, nb_ss, nb_rs,
):
    i = lax.axis_index("row")
    j = lax.axis_index("col")
    x = j // NZ
    z = lax.rem(j, NZ)
    q = i // 2
    core = lax.rem(i, 2)
    twin = (q * 2 + 1 - core, j)

    def row_peer(d):
        return (turn(i, d, NG), j)

    def col_peer(d):
        return (i, turn(j, d, NG))

    def x_peer(d):
        return (i, turn(x, d, NX) * NZ + z)

    def z_peer(d):
        return (i, x * NZ + turn(z, d, NZ))

    def tile_copy(c):
        part = pl.ds(c * (K // 4), K // 4)
        return pltpu.make_async_copy(tiles.at[0, 0, part], t.at[part], t_sem.at[c])

    for c in range(4):
        tile_copy(c).start()

    for buf in (ca, cb, na, nb):
        buf[...] = jnp.zeros_like(buf)

    barrier = pltpu.get_barrier_semaphore()

    def greet(device):
        pl.semaphore_signal(barrier, inc=1, device_id=device, device_id_type=MESH)

    repeat(NG - 1, lambda d: greet(row_peer(d + 1)))
    for d in FAR_FIRST:
        greet(x_peer(d + 1))
    for d in (0, 2):
        greet(z_peer(d + 1))

    def cut_dir(b):
        for r in range(RHS):
            dpiece[r, pl.ds(b, 1), :] = dirn[pl.ds(r, 1), pl.ds(pl.multiple_of(b * TB, TB), TB)]

    def cut_res(b):
        for r in range(RHS):
            rpiece[r, pl.ds(b, 1), :] = res[pl.ds(r, 1), pl.ds(pl.multiple_of(b * TB, TB), TB)]

    repeat(PC, cut_dir, unroll=4)
    xg[i] = dpiece[...].astype(BF16)
    repeat(PR, cut_res, unroll=4)
    rg[j] = rpiece[...].astype(BF16)

    pl.semaphore_wait(barrier, NG - 1 + NX - 1 + 2)
    pl.semaphore_signal(met, inc=1, device_id=z_peer(1), device_id_type=MESH)

    def send_x(d):
        peer = (turn(q, d + 1, NQ) * 2 + core, j)
        return remote(xg.at[i], xg.at[i], x_ss.at[d], x_rs.at[d], peer)

    def take_x(d):
        s = turn(q, -d - 1, NQ) * 2 + core
        return remote(xg.at[s], xg.at[s], x_ss.at[d], x_rs.at[d], twin)

    def send_twin(d):
        s = turn(q, -d, NQ) * 2 + core
        return remote(xg.at[s], xg.at[s], t_ss.at[d], t_rs.at[d], twin)

    def take_twin(d):
        s = turn(q, -d, NQ) * 2 + 1 - core
        return remote(xg.at[s], xg.at[s], t_ss.at[d], t_rs.at[d], twin)

    def z_send(buf, ss, rs, d):
        return remote(buf.at[j], buf.at[j], ss.at[d], rs.at[d], z_peer(d + 1))

    def z_take(buf, ss, rs, d):
        s = x * NZ + turn(z, -d - 1, NZ)
        return remote(buf.at[s], buf.at[s], ss.at[d], rs.at[d], z_peer(d + 1))

    def x_send(buf, ss, rs, e, d):
        s = x * NZ + turn(z, -e, NZ)
        return remote(buf.at[s], buf.at[s], ss.at[e, d], rs.at[e, d], x_peer(d + 1))

    def x_take(buf, ss, rs, e, d):
        s = turn(x, -d - 1, NX) * NZ + turn(z, -e, NZ)
        return remote(buf.at[s], buf.at[s], ss.at[e, d], rs.at[e, d], x_peer(d + 1))

    def gather_first(buf, zs, zr, xs, xr):
        for d in FAR_FIRST:
            z_send(buf, zs, zr, d).start()
        for d in FAR_FIRST:
            x_send(buf, xs, xr, 0, d).start()

    def gather_forward(buf, zs, zr, xs, xr):
        for d in FAR_LAST:
            z_take(buf, zs, zr, d).wait_recv()
            for f in FAR_FIRST:
                x_send(buf, xs, xr, d + 1, f).start()

    def gather_sent(buf, zs, zr, xs, xr):
        repeat(NZ - 1, lambda d: z_send(buf, zs, zr, d).wait_send())
        repeat(NZ, lambda e: repeat(NX - 1, lambda d: x_send(buf, xs, xr, e, d).wait_send()))

    repeat(NQ - 1, lambda d: send_x(d).start())
    send_twin(0).start()
    old = (rg, rz_ss, rz_rs, rx_ss, rx_rs)
    new = (ag, az_ss, az_rs, ax_ss, ax_rs)
    pl.semaphore_wait(met, 1)
    gather_first(*old)

    idx[...] = jnp.zeros_like(idx)
    idx[0:1, 0:K] = rows_v[0]
    idx[1:2, 0:K] = cols_v[0]
    count = count_s[0, 0]
    used = lax.broadcasted_iota(jnp.int32, (TB, KPAD), 1) < count
    down = lax.broadcasted_iota(jnp.int32, (TB, KPAD), 0)
    piece_row = (down // PR) * (NZ * PR) + down % PR
    for c in range(BR // TB):
        hit = jnp.where((piece_row + c * PR == idx[0:1, :]) & used, 1.0, 0.0).astype(BF16)
        hit_r[c * TB : (c + 1) * TB, 0:KPAD] = hit
        hit_r[c * TB : (c + 1) * TB, KPAD : 2 * KPAD] = hit
    for c in range(BC // TB):
        hit = jnp.where((down + c * TB == idx[1:2, :]) & used, 1.0, 0.0).astype(BF16)
        hit_c[c * TB : (c + 1) * TB, 0:KPAD] = hit
        hit_c[c * TB : (c + 1) * TB, KPAD : 2 * KPAD] = hit
    hilo[K:KPAD, :] = jnp.zeros((KPAD - K, RHS * TB), BF16)
    hilo[KPAD + K :, :] = jnp.zeros((KPAD - K, RHS * TB), BF16)

    top = lax.broadcasted_iota(jnp.int32, (8, TB), 0) < RHS
    slot = lax.broadcasted_iota(jnp.int32, (HALF, TB), 0)

    def spread(src, dst, p, blocks):
        at = pl.ds(pl.multiple_of(p * blocks, blocks), blocks)
        for r in range(RHS):
            v = src[p, r].astype(F32)
            dst[at, r, :] = v
            dst[at, RHS + r, :] = v

    def products(vec, index_s, transpose, between=None):
        axis = 0 if transpose else 1

        def four(k):
            v = [vec[index_s[0, 0, k + n * QUARTER]] for n in range(4)]
            lhs = jnp.concatenate(
                [
                    jnp.concatenate([jnp.where(top, v[n], 0.0), jnp.where(top, 0.0, v[n + 2])], axis=1)
                    for n in range(2)
                ],
                axis=0,
            )
            rhs = jnp.concatenate(
                [
                    jnp.concatenate([t[k + n * QUARTER], t[k + n * QUARTER + HALF]], axis=axis)
                    for n in range(2)
                ],
                axis=1 - axis,
            )
            y = lax.dot_general(
                lhs.astype(BF16), rhs, (((1,), (axis,)), ((), ())), preferred_element_type=F32
            )
            ys[k] = y[0:8, 0:TB]
            ys[k + QUARTER] = y[8:16, TB : 2 * TB]

        half = QUARTER // 2
        repeat(half, four, unroll=half)
        if between is not None:
            between()
        repeat(half, lambda k: four(k + half), unroll=half)
        for h in range(2):
            live = slot + h * HALF < count
            at = pl.ds(h * HALF, HALF)
            low_at = pl.ds(KPAD + h * HALF, HALF)
            for r in range(RHS):
                y = jnp.where(live, ys[:, h * RHS + r, :], 0.0)
                high = y.astype(BF16)
                hilo[at, r * TB : (r + 1) * TB] = high
                hilo[low_at, r * TB : (r + 1) * TB] = (y - high.astype(F32)).astype(BF16)

    def grad_chunk(buf, c):
        part = lax.dot_general(
            hit_c[c * TB : (c + 1) * TB, :], hilo[...], (((1,), (0,)), ((), ())),
            preferred_element_type=F32,
        )
        for n in range(TB // PC):
            for r in range(RHS):
                buf[c * (TB // PC) + n, r] = part[
                    n * PC : (n + 1) * PC, r * TB : (r + 1) * TB
                ].astype(BF16)

    def g_send(src, dst, ss, rs, d):
        return remote(src.at[turn(i, d + 1, NG)], dst.at[i], ss.at[d], rs.at[d], row_peer(d + 1))

    def g_sum(src, dst, ss, rs):
        def take(d):
            slot = dst.at[turn(i, -d - 1, NG)]
            remote(slot, slot, ss.at[d], rs.at[d], row_peer(d + 1)).wait_recv()

        repeat(NG - 1, take)
        dst[i] = src[i]
        total = dst[0].astype(F32)
        for n in range(1, NG):
            total += dst[n].astype(F32)
        return total

    g_old = (hs, hr, h_ss, h_rs)
    g_new = (gs, gr, g_ss, g_rs)

    def take_dir(d):
        take_x(d).wait_recv()
        send_twin(d + 1).start()
        spread(xg, xf, turn(q, -d - 1, NQ) * 2 + core, PC)

    def take_other(d):
        take_twin(d).wait_recv()
        spread(xg, xf, turn(q, -d, NQ) * 2 + 1 - core, PC)

    spread(xg, xf, i, PC)
    repeat(NQ - 1, take_dir)
    gather_forward(*old)
    repeat(NQ, take_other)
    for c in range(4):
        tile_copy(c).wait()
    products(xf, cols_s, False)

    def s1_send(d, e):
        p = turn(x, d + 1, NX) * NZ + turn(z, e + 1, NZ)
        dst = r1.at[turn(z, e + 1, NZ), x]
        return remote(sb.at[p], dst, s1_ss.at[d, e], s1_rs.at[d, e], x_peer(d + 1))

    def s1_take(d, e):
        dst = r1.at[turn(z, e + 1, NZ), turn(x, -d - 1, NX)]
        return remote(dst, dst, s1_ss.at[d, e], s1_rs.at[d, e], x_peer(d + 1))

    def s2_send(e):
        return remote(
            sb.at[x * NZ + turn(z, e + 1, NZ)], r2.at[z], s2_ss.at[e], s2_rs.at[e], z_peer(e + 1)
        )

    def s2_take(e):
        dst = r2.at[turn(z, -e - 1, NZ)]
        return remote(dst, dst, s2_ss.at[e], s2_rs.at[e], z_peer(e + 1))

    def image_chunk(e):
        ze = turn(z, e + 1, NZ)
        hit = hit_r[pl.ds(pl.multiple_of(ze * TB, TB), TB), :]
        part = lax.dot_general(hit, hilo[...], (((1,), (0,)), ((), ())), preferred_element_type=F32)
        for n in range(NX):
            for r in range(RHS):
                sb[n * NZ + ze, r] = part[n * PR : (n + 1) * PR, r * TB : (r + 1) * TB].astype(BF16)

    for e in FAR_FIRST + (NZ - 1,):
        image_chunk(e)
        for d in FAR_FIRST:
            s1_send(d, e).start()

    def over_x(e):
        zt = turn(z, e + 1, NZ)
        repeat(NX - 1, lambda d: s1_take(d, e).wait_recv())
        total = sb[x * NZ + zt].astype(F32)
        for d in range(NX - 1):
            total += r1[zt, turn(x, -d - 1, NX)].astype(F32)
        return total

    def through(e):
        sb[x * NZ + turn(z, e + 1, NZ)] = over_x(e).astype(BF16)
        s2_send(e).start()

    for e in FAR_FIRST:
        through(e)
    image[...] = over_x(NZ - 1)

    spread(rg, rf, j, PR)

    def take_res(e):
        def one(d):
            x_take(*((rg,) + old[3:]), e, d).wait_recv()
            spread(rg, rf, turn(x, -d - 1, NX) * NZ + turn(z, -e, NZ), PR)

        repeat(NX - 1, one)

    repeat(NZ, take_res)
    repeat(NZ - 1, lambda d: spread(rg, rf, x * NZ + turn(z, -d - 1, NZ), PR))
    products(rf, rows_s, True)
    for c in range(BC // TB):
        grad_chunk(hs, c)

    def add_image(e):
        s2_take(e).wait_recv()
        image[...] += r2[turn(z, -e - 1, NZ)].astype(F32)

    for e in FAR_LAST:
        add_image(e)

    ag[j] = image[...].astype(BF16)
    gather_first(*new)

    def share(buf, me, peer, ss, rs):
        return lambda d: remote(buf.at[me], buf.at[me], ss.at[d], rs.at[d], peer(d + 1))

    def shared(buf, me, peer, ss, rs):
        def take(d):
            s = turn(me, -d - 1, NG)
            remote(buf.at[s], buf.at[s], ss.at[d], rs.at[d], peer(d + 1)).wait_recv()

        repeat(NG - 1, take)
        return jnp.sum(buf[...], axis=0)

    for r in range(RHS):
        v = image[r]
        ca[j, r : r + 1, :] = jnp.sum(v * v, axis=0, keepdims=True)
    c_col = (ca, j, col_peer, ca_ss, ca_rs)
    c_row = (cb, i, row_peer, cb_ss, cb_rs)
    repeat(NG - 1, lambda d: share(*c_col)(d).start())
    gather_forward(*new)
    repeat(NG - 1, lambda d: g_send(*g_old, d).start())

    def write_image(b):
        for r in range(RHS):
            at = pl.ds(pl.multiple_of(b * TB, TB), TB)
            out_image[pl.ds(r, 1), at] = image[r, pl.ds(b, 1), :]

    repeat(PR, write_image, unroll=4)
    line = lax.broadcasted_iota(jnp.int32, (RHS, 1), 0)
    gamma = jnp.full((RHS, 1), gamma_s[0], F32)
    for r in range(1, RHS):
        gamma = jnp.where(line == r, gamma_s[r], gamma)

    spread(ag, rf, j, PR)
    repeat(NZ - 1, lambda d: spread(ag, rf, x * NZ + turn(z, -d - 1, NZ), PR))

    def take_image(e):
        def one(d):
            x_take(*((ag,) + new[3:]), e, d).wait_recv()
            spread(ag, rf, turn(x, -d - 1, NX) * NZ + turn(z, -e, NZ), PR)

        repeat(NX - 1, one)

    for e in (0, 1, 3):
        take_image(e)
    cb[i] = shared(*c_col)
    repeat(NG - 1, lambda d: share(*c_row)(d).start())
    take_image(2)
    products(rf, rows_s, True)

    for c in range(BC // TB):
        grad_chunk(gs, c)
    repeat(NG - 1, lambda d: g_send(*g_new, d).start())

    grad_r[...] = g_sum(*g_old)
    curvature = jnp.sum(shared(*c_row)[0:RHS, :], axis=1, keepdims=True)
    step = gamma / curvature
    out_scale[0] = jnp.broadcast_to(step, (RHS, TB))
    total = g_sum(*g_new)
    grad = [grad_r[r] - step[r : r + 1, :] * total[r] for r in range(RHS)]

    for r in range(RHS):
        v = grad[r]
        na[i, r : r + 1, :] = jnp.sum(v * v, axis=0, keepdims=True)
    n_row = (na, i, row_peer, na_ss, na_rs)
    n_col = (nb, j, col_peer, nb_ss, nb_rs)
    repeat(NG - 1, lambda d: share(*n_row)(d).start())
    for r in range(RHS):
        for b in range(PC):
            out_grad[r : r + 1, b * TB : (b + 1) * TB] = grad[r][b : b + 1, :]
    repeat(NQ - 1, lambda d: send_x(d).wait_send())
    repeat(NQ, lambda d: send_twin(d).wait_send())
    gather_sent(*old)
    repeat(NX - 1, lambda d: repeat(NZ, lambda e: s1_send(d, e).wait_send()))
    repeat(NZ - 1, lambda e: s2_send(e).wait_send())
    nb[j] = shared(*n_row)
    repeat(NG - 1, lambda d: share(*n_col)(d).start())
    gather_sent(*new)
    repeat(NG - 1, lambda d: share(*c_col)(d).wait_send())
    repeat(NG - 1, lambda d: share(*c_row)(d).wait_send())
    repeat(NG - 1, lambda d: g_send(*g_old, d).wait_send())
    repeat(NG - 1, lambda d: g_send(*g_new, d).wait_send())
    repeat(NG - 1, lambda d: share(*n_row)(d).wait_send())
    norm_next = jnp.sum(shared(*n_col)[0:RHS, :], axis=1, keepdims=True)
    out_scale[1] = jnp.broadcast_to(norm_next / gamma, (RHS, TB))

    repeat(NG - 1, lambda d: share(*n_col)(d).wait_send())


def finish(sol, res, dirn, image, gradient, scale, out_sol, out_res, out_dir):
    step = scale[0, :, 0:1]
    beta = scale[1, :, 0:1]
    out_sol[...] = sol[...] + step * dirn[...]
    out_res[...] = res[...] - step * image[...]
    out_dir[...] = gradient[...] + beta * dirn[...]


def on_device(
    tile_values, tile_rows, tile_cols, tile_counts, solution, residual, direction, grad_norm
):
    smem = pl.BlockSpec(memory_space=pltpu.SMEM)
    vmem = pl.BlockSpec(memory_space=pltpu.VMEM)
    piece_r = (RHS, PR, TB)
    piece_c = (RHS, PC, TB)
    dma = pltpu.SemaphoreType.DMA
    peers = [dma((NG - 1,)), dma((NG - 1,))]
    staged = [dma((NZ - 1,)), dma((NZ - 1,)), dma((NZ, NX - 1)), dma((NZ, NX - 1))]
    image, gradient, scale = pl.pallas_call(
        kernel,
        out_shape=(
            jax.ShapeDtypeStruct(residual.shape, F32),
            jax.ShapeDtypeStruct(direction.shape, F32),
            jax.ShapeDtypeStruct((2, RHS, TB), F32),
        ),
        in_specs=[smem, smem, smem, smem, vmem, vmem, pl.BlockSpec(memory_space=pltpu.HBM)]
        + [vmem] * 2,
        out_specs=(vmem, vmem, vmem),
        scratch_shapes=[
            pltpu.VMEM((K, TB, TB), BF16),
            pltpu.VMEM((NG,) + piece_c, BF16),
            pltpu.VMEM((NG,) + piece_r, BF16),
            pltpu.VMEM((NG,) + piece_r, BF16),
            pltpu.VMEM((NG,) + piece_r, BF16),
            pltpu.VMEM((NZ, NX) + piece_r, BF16),
            pltpu.VMEM((NZ,) + piece_r, BF16),
            pltpu.VMEM((NG,) + piece_c, BF16),
            pltpu.VMEM((NG,) + piece_c, BF16),
            pltpu.VMEM((NG,) + piece_c, BF16),
            pltpu.VMEM((NG,) + piece_c, BF16),
            pltpu.VMEM(piece_c, F32),
            pltpu.VMEM(piece_r, F32),
            pltpu.VMEM(piece_r, F32),
            pltpu.VMEM((BC, 2 * RHS, TB), F32),
            pltpu.VMEM((BR, 2 * RHS, TB), F32),
            pltpu.VMEM((HALF, 2 * RHS, TB), F32),
            pltpu.VMEM((2 * KPAD, RHS * TB), BF16),
            pltpu.VMEM((BR, 2 * KPAD), BF16),
            pltpu.VMEM((BC, 2 * KPAD), BF16),
            pltpu.VMEM(piece_c, F32),
            pltpu.VMEM((8, KPAD), jnp.int32),
            pltpu.VMEM((NG, 8, TB), F32),
            pltpu.VMEM((NG, 8, TB), F32),
            pltpu.VMEM((NG, 8, TB), F32),
            pltpu.VMEM((NG, 8, TB), F32),
            pltpu.SemaphoreType.REGULAR,
            dma((4,)),
            dma((NQ - 1,)), dma((NQ - 1,)),
            dma((NQ,)), dma((NQ,)),
            *staged,
            dma((NX - 1, NZ)), dma((NX - 1, NZ)),
            dma((NZ - 1,)), dma((NZ - 1,)),
            *staged,
            *peers,
            *peers,
            *peers, *peers, *peers, *peers,
        ],
        compiler_params=pltpu.CompilerParams(
            collective_id=0, has_side_effects=True, vmem_limit_bytes=60 * 1024 * 1024
        ),
    )(
        tile_counts, tile_rows, tile_cols, grad_norm, tile_rows, tile_cols,
        tile_values, residual, direction,
    )
    return pl.pallas_call(
        finish,
        out_shape=tuple(
            jax.ShapeDtypeStruct(a.shape, F32) for a in (solution, residual, direction)
        ),
        in_specs=[vmem] * 6,
        out_specs=(vmem, vmem, vmem),
    )(solution, residual, direction, image, gradient, scale)


def solution(mesh):
    in_specs = (
        P("row", "col", None, None, None),
        P("row", "col", None),
        P("row", "col", None),
        P("row", "col"),
        P(None, ("col", "row")),
        P(None, ("row", "col")),
        P(None, ("col", "row")),
        P(),
    )
    out_specs = (P(None, ("col", "row")), P(None, ("row", "col")), P(None, ("col", "row")))
    return jax.shard_map(
        on_device, mesh=mesh, in_specs=in_specs, out_specs=out_specs, check_vma=False
    )
```
